32 devices in a mesh: req: 16 (over z, x, core), ctx: 2 (over y).
Axes of the slice: x: 2, y: 2, z: 4, core: 2. Of those that a mesh axis runs over, the one named last changes fastest.
Arguments:
- q_heads: bfloat16 [16, 256, 12288], P('req', 'ctx'), may hold values from -204 to 204
- kv_latent: bfloat16 [16, 256, 576], P('req', 'ctx'), may hold values from -600 to 600
- latent_gain: float32 [512], replicated, may hold values from 0.1 to 1.9
- kv_up: bfloat16 [64, 256, 512], P('ctx'), may hold values from -0.25 to 0.25
- offsets: int32 [16], P('req'), may hold values from 0 to 1792, as said below
- lengths: int32 [16], P('req'), may hold values from 64 to 256
- block_order: int32 [16, 4], P('req'), may hold values from 0 to 3, each once within a row
- owners: int32 [16, 4], P(None, 'ctx'), may hold values from 0 to 15, as said below
Outputs:
- attn_out: bfloat16 [16, 256, 8192], P('req', 'ctx')
- shipped: bfloat16 [16, 4, 36864], P('req', 'ctx')
The draws below stay inside these ranges and needn't reach their ends.
Inputs may be any that keep to these rules, and one draw needn't show every extreme that they name: `offsets`: each entry is a multiple of 256. `block_order`: each row names every block index once. `owners`: for each context index j, column 2 j and column 2 j + 1 each name every owner once, and no row names the same owner in both of them.
All inputs are finite; a program needn't handle non-finite values.
Results may differ from the reference program's by a relative error of at most 0.007.
Values may be sent and summed in bfloat16 or wider, within the bound.
A program may use at most 64 MiB of HBM per device.

```python
import math
import jax
import jax.numpy as jnp
from jax import lax

HEADS = 64
HD = 128
ROPE = 64
LAT = 512
SEGMENTS = 8
BLK = 64
SEGLEN = 256
REQS = 16
KVW = 576
N_CTX = 2


def draw_q_heads(key, part):
    subkeys = jax.random.split(key, 1)
    shape_full = (REQS, SEGLEN, HEADS * (HD + ROPE))
    values = jnp.clip(jax.random.normal(subkeys[0], shape_full, jnp.float32), -6.0, 6.0)
    return values.astype(jnp.bfloat16)


def draw_kv_latent(key, part):
    subkeys = jax.random.split(key, 5)
    shape_latent = (REQS, SEGLEN, LAT)
    row_scale = jnp.exp(jax.random.uniform(subkeys[0], (REQS, SEGLEN, 1), jnp.float32, 0.0, math.log(10.0)))
    column_scale = jnp.exp(jax.random.uniform(subkeys[1], (1, 1, LAT), jnp.float32, 0.0, math.log(10.0)))
    latent = jnp.clip(jax.random.normal(subkeys[3], shape_latent, jnp.float32), -6.0, 6.0) * row_scale * column_scale
    rope_part = jnp.clip(jax.random.normal(subkeys[4], (REQS, SEGLEN, ROPE), jnp.float32), -6.0, 6.0)
    values = jnp.clip(jnp.concatenate([latent, rope_part], axis=-1), -600.0, 600.0)
    return values.astype(jnp.bfloat16)


def draw_offsets(key, part):
    subkeys = jax.random.split(key, 2)
    values = SEGLEN * jax.random.randint(subkeys[0], (REQS,), 0, SEGMENTS)
    picked = jax.random.permutation(subkeys[1], REQS)
    values = values.at[picked[0]].set(0).at[picked[1]].set((SEGMENTS - 1) * SEGLEN)
    return values.astype(jnp.int32)


def draw_lengths(key, part):
    subkeys = jax.random.split(key, 2)
    values = jax.random.randint(subkeys[0], (REQS,), BLK, SEGLEN + 1)
    picked = jax.random.permutation(subkeys[1], REQS)
    values = values.at[picked[0]].set(SEGLEN).at[picked[1]].set(BLK)
    return values.astype(jnp.int32)


def draw_owners(key, part):
    columns = []
    for context in range(N_CTX):
        subkeys = jax.random.split(jax.random.fold_in(key, 7 + context), 2)
        first_owner = jax.random.permutation(subkeys[0], REQS).astype(jnp.int32)
        shift_by = jax.random.randint(subkeys[1], (), 1, REQS)
        second_owner = first_owner[(jnp.arange(REQS, dtype=jnp.int32) + shift_by) % REQS]
        columns.append(first_owner)
        columns.append(second_owner)
    return jnp.stack(columns, axis=1).astype(jnp.int32)


def block_levels(own_key, extent, cuts, low, high):
    factor_of, own = 1.0, jax.random.fold_in(own_key, 6)
    for axis_at, blocks in cuts:
        draws = jnp.exp(jax.random.uniform(jax.random.fold_in(own, axis_at), (blocks,), jnp.float32, low / len(cuts), high / len(cuts)))
        factor_of = factor_of * jnp.repeat(draws, extent[axis_at] // blocks).reshape([-1 if axis == axis_at else 1 for axis in range(len(extent))])
    return factor_of


def bell_draw(key, shape, deviation, reach, cuts=(), held_as=jnp.bfloat16):
    loudness = block_levels(key, shape, cuts, -0.22, 0.18) if cuts else 1.0
    entries = jax.random.normal(key, shape, jnp.float32) * deviation * loudness
    return jnp.minimum(jnp.maximum(entries, -reach), reach).astype(held_as)


def setup_inputs(seed: int = 0) -> dict:
    key_list = jax.random.split(jax.random.key(seed), 9)
    return {
        "q_heads": draw_q_heads(jax.random.fold_in(key_list[8], 71), 0),
        "kv_latent": draw_kv_latent(jax.random.fold_in(key_list[8], 71), 0),
        "latent_gain": jnp.clip(1.0 + 0.18 * jax.random.normal(key_list[2], (LAT,), jnp.float32), 0.1, 1.9),
        "kv_up": bell_draw(key_list[3], (HEADS, 2 * HD, LAT), LAT ** -0.5, 0.25, ((0, 2),)),
        "offsets": draw_offsets(jax.random.fold_in(key_list[8], 71), 0),
        "lengths": draw_lengths(jax.random.fold_in(key_list[8], 71), 0),
        "block_order": jax.vmap(lambda own: jax.random.permutation(own, 2 * N_CTX))(jax.random.split(key_list[6], REQS)).reshape((REQS, 2 * N_CTX)).astype(jnp.int32),
        "owners": draw_owners(jax.random.fold_in(key_list[8], 71), 0),
    }


theta_base = 10000.0
epsilon = 1e-06
masked_fill = -1e+30

def rotate(values, angles):
    half_width = values.shape[-1] // 2
    first_half = values[..., :half_width]
    second_half = values[..., half_width:]
    cosine = jnp.cos(angles)
    sine_part = jnp.sin(angles)
    return jnp.concatenate([first_half * cosine - second_half * sine_part, second_half * cosine + first_half * sine_part], axis=-1)

def angle_table(positions, rope_width):
    half_width = rope_width // 2
    frequency = jnp.exp(-math.log(theta_base) * jnp.arange(half_width, dtype=jnp.float32) / half_width)
    return positions.astype(jnp.float32)[:, None] * frequency[None, :]

def make_cache(latent_rows, latent_gain, angles):
    latent = latent_rows[:, :LAT].astype(jnp.float32)
    mean_square = lax.optimization_barrier(jnp.mean(latent * latent, axis=-1, keepdims=True))
    normed = (latent * lax.rsqrt(mean_square + epsilon) * latent_gain).astype(jnp.bfloat16)
    key_rope = rotate(latent_rows[:, LAT:].astype(jnp.float32), angles).astype(jnp.bfloat16)
    return jnp.concatenate([normed, key_rope], axis=-1)

def attend(queries, key_rows, value_weight, allowed, valid_rows):
    score_scale = (HD + ROPE) ** (-0.5)
    scores = jnp.dot(queries, key_rows.T, preferred_element_type=jnp.float32) * score_scale
    masked = jnp.where(allowed, scores, masked_fill)
    row_max = lax.optimization_barrier(jnp.max(masked, axis=-1, keepdims=True))
    exponent = jnp.exp(masked - row_max)
    probabilities = (exponent / lax.optimization_barrier(jnp.sum(exponent, axis=-1, keepdims=True))).astype(jnp.bfloat16)
    output_latent = jnp.dot(probabilities, key_rows[:, :LAT], preferred_element_type=jnp.float32).astype(jnp.bfloat16)
    projected = jnp.dot(output_latent, value_weight.T, preferred_element_type=jnp.float32)
    return jnp.where(valid_rows[:, None], projected, 0.0).astype(jnp.bfloat16)

def reference(q_heads, kv_latent, latent_gain, kv_up, offsets, lengths, block_order, owners):
    segment_rows = jnp.arange(SEGLEN, dtype=jnp.int32)

    def one_request(request):
        positions = block_order[request][segment_rows // BLK] * BLK + segment_rows % BLK
        angles = angle_table(offsets[request] + positions, ROPE)
        cache_rows = make_cache(kv_latent[request], latent_gain, angles)
        query_parts = q_heads[request].reshape(SEGLEN, HEADS, HD + ROPE)
        query_rope = rotate(query_parts[:, :, HD:].astype(jnp.float32), angles[:, None, :]).astype(jnp.bfloat16)
        allowed = (positions[None, :] <= positions[:, None]) & (positions[None, :] < lengths[request])
        valid_rows = positions < lengths[request]

        def one_head(head_index):
            weight = kv_up[head_index]
            query_latent = jnp.dot(query_parts[:, head_index, :HD], weight[:HD], preferred_element_type=jnp.float32).astype(jnp.bfloat16)
            queries = jnp.concatenate([query_latent, query_rope[:, head_index]], axis=-1)
            return attend(queries, cache_rows, weight[HD:], allowed, valid_rows)
        per_head = lax.map(one_head, jnp.arange(HEADS, dtype=jnp.int32))
        return (per_head.transpose(1, 0, 2).reshape(SEGLEN, HEADS * HD), cache_rows)
    attn_out, caches = lax.map(one_request, jnp.arange(REQS, dtype=jnp.int32))
    page_rows = caches.reshape(REQS, N_CTX, 2, BLK * KVW)
    source_index = jnp.arange(2 * REQS, dtype=jnp.int32)
    owner_index = jnp.arange(REQS, dtype=jnp.int32)
    columns = []
    for context in range(N_CTX):
        named_owner = owners[:, 2 * context:2 * context + 2].reshape(2 * REQS)
        matches = named_owner[None, :] == owner_index[:, None]
        first_slot = lax.optimization_barrier(jnp.min(jnp.where(matches, source_index[None, :], 2 * REQS), axis=1))
        second_slot = lax.optimization_barrier(jnp.min(jnp.where(matches & (source_index[None, :] != first_slot[:, None]), source_index[None, :], 2 * REQS), axis=1))
        candidates = page_rows[:, context].reshape(2 * REQS, BLK * KVW)
        columns.append(jnp.stack([candidates[first_slot], candidates[second_slot]], axis=1))
    shipped = jnp.stack(columns, axis=1).reshape(REQS, N_CTX * 2, BLK * KVW)
    return (attn_out, shipped)
```

```python
import functools
import math

import jax
import jax.numpy as jnp
from jax import lax
from jax.experimental import pallas as pl
from jax.experimental.pallas import tpu as pltpu
from jax.sharding import PartitionSpec as P

HEADS = 64
HD = 128
ROPE = 64
LAT = 512
QW = HD + ROPE

theta_base = 10000.0
epsilon = 1e-06
masked_fill = -1e30
MESH = pl.DeviceIdType.MESH


def row_positions(order_ref, shape, axis, block_width, blocks):
    index = lax.broadcasted_iota(jnp.int32, shape, axis)
    block = index // block_width
    position = index - block * block_width
    for j in range(blocks):
        position = position + jnp.where(block == j, order_ref[0, j] * block_width, 0)
    return position


def attention_kernel(
    groups,
    chunk_heads,
    order_ref,
    length_ref,
    q_hbm,
    cache_ref,
    cos_ref,
    sin_ref,
    w_hbm,
    out_hbm,
    qbuf,
    wbuf,
    keys,
    cache_t,
    rope_t,
    bias,
    obuf,
    w_sem,
    qown_sem,
    oown_sem,
    key_send,
    key_recv,
    q_send,
    q_recv,
    o_send,
    o_recv,
):
    me = lax.axis_index("ctx")
    rows = q_hbm.shape[0]
    segment = rows * groups
    heads = w_hbm.shape[0]
    chunks = heads // chunk_heads
    q_width = chunk_heads * QW
    o_width = chunk_heads * HD
    blocks = order_ref.shape[1]
    block_width = segment // blocks

    def peer(step):
        return lax.rem(me + step, groups)

    def own_rows(index):
        return pl.ds(pl.multiple_of(index * rows, rows), rows)

    def q_columns(group, c):
        return pl.ds(pl.multiple_of(group * (heads * QW) + c * q_width, 128), q_width)

    def o_columns(group, c):
        return pl.ds(pl.multiple_of(group * (heads * HD) + c * o_width, 128), o_width)

    def key_copy(step):
        return pltpu.make_async_remote_copy(
            src_ref=cache_ref,
            dst_ref=keys.at[own_rows(me)],
            send_sem=key_send.at[step - 1],
            recv_sem=key_recv.at[step - 1],
            device_id={"ctx": peer(step)},
            device_id_type=MESH,
        )

    def q_copy(step, c):
        return pltpu.make_async_remote_copy(
            src_ref=q_hbm.at[:, q_columns(peer(step), c)],
            dst_ref=qbuf.at[c, own_rows(me)],
            send_sem=q_send.at[step - 1, c],
            recv_sem=q_recv.at[step - 1, c],
            device_id={"ctx": peer(step)},
            device_id_type=MESH,
        )

    def o_copy(step, c):
        return pltpu.make_async_remote_copy(
            src_ref=obuf.at[c, own_rows(peer(step))],
            dst_ref=out_hbm.at[:, o_columns(me, c)],
            send_sem=o_send.at[step - 1, c],
            recv_sem=o_recv.at[step - 1, c],
            device_id={"ctx": peer(step)},
            device_id_type=MESH,
        )

    def q_own(c):
        return pltpu.make_async_copy(
            q_hbm.at[:, q_columns(me, c)], qbuf.at[c, own_rows(me)], qown_sem.at[c]
        )

    def w_copy(c):
        return pltpu.make_async_copy(
            w_hbm.at[pl.ds(c * chunk_heads, chunk_heads)], wbuf.at[c], w_sem.at[c]
        )

    def o_own(c):
        return pltpu.make_async_copy(
            obuf.at[c, own_rows(me)], out_hbm.at[:, o_columns(me, c)], oown_sem.at[c]
        )

    barrier = pltpu.get_barrier_semaphore()
    for step in range(1, groups):
        pl.semaphore_signal(
            barrier, inc=1, device_id={"ctx": peer(step)}, device_id_type=MESH
        )
    pl.semaphore_wait(barrier, groups - 1)

    for step in range(1, groups):
        key_copy(step).start()
    for c in range(chunks):
        for step in range(1, groups):
            q_copy(step, c).start()
    for c in range(chunks):
        w_copy(c).start()
        q_own(c).start()

    keys[own_rows(me)] = cache_ref[...]
    length = length_ref[0]
    query_pos = row_positions(order_ref, (segment, 1), 0, block_width, blocks)
    key_pos = row_positions(order_ref, (1, segment), 1, block_width, blocks)
    bias[...] = jnp.where((key_pos <= query_pos) & (key_pos < length), 0.0, masked_fill)

    for step in range(1, groups):
        key_copy(step).wait()
    for g in range(groups):
        span = slice(g * rows, (g + 1) * rows)
        cache_t[:, span] = keys[span, :LAT].astype(jnp.float32).T.astype(jnp.bfloat16)
        turned = keys[span, LAT:].astype(jnp.float32)
        empty = jnp.zeros_like(turned)
        rope_t[0, :, span] = jnp.concatenate([turned, empty], axis=1).T.astype(jnp.bfloat16)
        rope_t[1, :, span] = jnp.concatenate([empty, turned], axis=1).T.astype(jnp.bfloat16)

    scale = (QW ** -0.5) * math.log2(math.e)
    tile = min(256, segment)
    lane = lax.broadcasted_iota(jnp.int32, (tile, 128), 1)
    low = lane < ROPE
    first = (lane & (ROPE // 2)) == 0

    def one_chunk(c, carry):
        w_copy(c).wait()
        q_own(c).wait()
        for step in range(1, groups):
            q_copy(step, c).wait()
        weights = wbuf[c].reshape(chunk_heads * 2 * HD, LAT)
        expanded = jnp.dot(
            weights, cache_t[...], preferred_element_type=jnp.float32
        ).astype(jnp.bfloat16)
        ones = jnp.ones((HD, segment), jnp.bfloat16)
        for t in range(segment // tile):
            span = slice(t * tile, (t + 1) * tile)
            valid = (
                row_positions(order_ref, (tile, HD), 0, block_width, blocks)
                if segment == tile
                else None
            )
            if valid is None:
                index = lax.broadcasted_iota(jnp.int32, (tile, HD), 0) + t * tile
                block = index // block_width
                valid = index - block * block_width
                for j in range(blocks):
                    valid = valid + jnp.where(block == j, order_ref[0, j] * block_width, 0)
            valid = valid < length
            for pair in range(chunk_heads // 2):
                at = pair * 2 * QW
                part0 = qbuf[c, span, at : at + 128]
                part1 = qbuf[c, span, at + 128 : at + 256].astype(jnp.float32)
                part2 = qbuf[c, span, at + 256 : at + 384].astype(jnp.float32)
                plain = jnp.where(low, part1, part2)
                other = jnp.where(
                    first,
                    pltpu.roll(plain, 128 - ROPE // 2, 1),
                    pltpu.roll(plain, ROPE // 2, 1),
                )
                turned = (plain * cos_ref[span] + other * sin_ref[span]).astype(jnp.bfloat16)
                swapped = jnp.where(low, part2, part1).astype(jnp.bfloat16)
                for odd in range(2):
                    top = (pair * 2 + odd) * 2 * HD
                    key_t = expanded[top : top + HD]
                    value_t = expanded[top + HD : top + 2 * HD]
                    if odd:
                        key_t = jnp.concatenate(
                            [key_t[HD // 2 :], key_t[: HD // 2], rope_t[1]], axis=0
                        )
                        query = jnp.concatenate([swapped, turned], axis=1)
                    else:
                        key_t = jnp.concatenate([key_t, rope_t[0]], axis=0)
                        query = jnp.concatenate([part0, turned], axis=1)
                    scores = (
                        jnp.dot(query, key_t, preferred_element_type=jnp.float32) * scale
                        + bias[span]
                    )
                    top_score = jnp.max(scores, axis=-1, keepdims=True)
                    weight = jnp.exp2(scores - top_score).astype(jnp.bfloat16)
                    summed = lax.dot_general(
                        weight,
                        jnp.concatenate([value_t, ones], axis=0),
                        (((1,), (1,)), ((), ())),
                        preferred_element_type=jnp.float32,
                    )
                    result = jnp.where(valid, summed[:, :HD] / summed[:, HD:], 0.0)
                    column = (pair * 2 + odd) * HD
                    obuf[c, span, column : column + HD] = result.astype(jnp.bfloat16)
        for step in range(1, groups):
            o_copy(step, c).start()
        o_own(c).start()
        return carry

    lax.fori_loop(0, chunks, one_chunk, 0)

    def finish(c, carry):
        o_own(c).wait()
        for step in range(1, groups):
            o_copy(step, c).wait()
        return carry

    lax.fori_loop(0, chunks, finish, 0)


def attention(q, cache_rows, cosine, sine, kv_up, order, length):
    groups = lax.axis_size("ctx")
    rows = q.shape[0]
    segment = rows * groups
    heads = kv_up.shape[0]
    chunk_heads = min(4, heads)
    chunks = heads // chunk_heads
    in_vmem = pl.BlockSpec(memory_space=pltpu.VMEM)
    in_smem = pl.BlockSpec(memory_space=pltpu.SMEM)
    anywhere = pl.BlockSpec(memory_space=pl.ANY)
    dma = pltpu.SemaphoreType.DMA
    others = groups - 1
    return pl.pallas_call(
        functools.partial(attention_kernel, groups, chunk_heads),
        out_shape=jax.ShapeDtypeStruct((rows, HEADS * HD), jnp.bfloat16),
        in_specs=[in_smem, in_smem, anywhere, in_vmem, in_vmem, in_vmem, anywhere],
        out_specs=anywhere,
        scratch_shapes=[
            pltpu.VMEM((chunks, segment, chunk_heads * QW), jnp.bfloat16),
            pltpu.VMEM((chunks, chunk_heads, 2 * HD, LAT), jnp.bfloat16),
            pltpu.VMEM((segment, LAT + ROPE), jnp.bfloat16),
            pltpu.VMEM((LAT, segment), jnp.bfloat16),
            pltpu.VMEM((2, 2 * ROPE, segment), jnp.bfloat16),
            pltpu.VMEM((segment, segment), jnp.float32),
            pltpu.VMEM((chunks, segment, chunk_heads * HD), jnp.bfloat16),
            dma((chunks,)),
            dma((chunks,)),
            dma((chunks,)),
            dma((others,)),
            dma((others,)),
            dma((others, chunks)),
            dma((others, chunks)),
            dma((others, chunks)),
            dma((others, chunks)),
        ],
        compiler_params=pltpu.CompilerParams(
            collective_id=0, has_side_effects=True, vmem_limit_bytes=52 * 2**20
        ),
        cost_estimate=pl.CostEstimate(
            flops=2 * heads * segment * (2 * HD * LAT + 4 * HD * segment),
            bytes_accessed=2 * (2 * rows * HEADS * QW + heads * 2 * HD * LAT + rows * HEADS * HD),
            transcendentals=heads * segment * segment,
        ),
    )(order, length, q, cache_rows, cosine, sine, kv_up)


def per_device(q_heads, kv_latent, latent_gain, kv_up, offsets, lengths, block_order, owners):
    groups = lax.axis_size("ctx")
    context = lax.axis_index("ctx")
    local_rows = q_heads.shape[1]
    segment = local_rows * groups
    blocks = block_order.shape[1]
    block_width = segment // blocks
    order_row = block_order[0]
    positions = (
        order_row[:, None] * block_width + jnp.arange(block_width, dtype=jnp.int32)[None, :]
    ).reshape(segment)
    half = ROPE // 2
    frequency = jnp.exp(-math.log(theta_base) * jnp.arange(half, dtype=jnp.float32) / half)
    angles = (offsets[0] + positions).astype(jnp.float32)[:, None] * frequency[None, :]
    cosine = jnp.cos(angles)
    sine = jnp.sin(angles)
    latent_rows = kv_latent[0]
    latent = latent_rows[:, :LAT].astype(jnp.float32)
    mean_square = jnp.mean(latent * latent, axis=-1, keepdims=True)
    normed = (latent * lax.rsqrt(mean_square + epsilon) * latent_gain).astype(jnp.bfloat16)
    cos_here = lax.dynamic_slice_in_dim(cosine, context * local_rows, local_rows)
    sin_here = lax.dynamic_slice_in_dim(sine, context * local_rows, local_rows)
    first = latent_rows[:, LAT : LAT + half].astype(jnp.float32)
    second = latent_rows[:, LAT + half :].astype(jnp.float32)
    key_rope = jnp.concatenate(
        [first * cos_here - second * sin_here, second * cos_here + first * sin_here], axis=-1
    ).astype(jnp.bfloat16)
    cache_rows = jnp.concatenate([normed, key_rope], axis=-1)

    page_rows = cache_rows.reshape(local_rows // block_width, block_width * cache_rows.shape[1])
    everyone = lax.all_gather(page_rows, "req", axis=0, tiled=True)

    attn_out = attention(
        q_heads[0],
        cache_rows,
        jnp.concatenate([cosine] * 4, axis=1),
        jnp.concatenate([-sine, sine, -sine, sine], axis=1),
        kv_up,
        block_order,
        lengths,
    )

    owner_here = lax.axis_index("req")
    named_owner = owners.reshape(-1)
    source_index = jnp.arange(named_owner.shape[0], dtype=jnp.int32)
    matches = named_owner == owner_here
    first_slot = jnp.min(jnp.where(matches, source_index, named_owner.shape[0]))
    second_slot = jnp.max(jnp.where(matches, source_index, -1))
    shipped = jnp.concatenate(
        [
            lax.dynamic_slice_in_dim(everyone, first_slot, 1),
            lax.dynamic_slice_in_dim(everyone, second_slot, 1),
        ],
        axis=0,
    )
    return (attn_out[None], shipped[None])


def solution(mesh):
    in_specs = (
        P("req", "ctx", None),
        P("req", "ctx", None),
        P(),
        P("ctx", None, None),
        P("req"),
        P("req"),
        P("req", None),
        P(None, "ctx"),
    )
    out_specs = (P("req", "ctx", None), P("req", "ctx", None))
    return jax.shard_map(
        per_device, mesh=mesh, in_specs=in_specs, out_specs=out_specs, check_vma=False
    )
```

```python
import functools
import math

import jax
import jax.numpy as jnp
import numpy as np
from jax import lax
from jax.experimental import pallas as pl
from jax.experimental.pallas import tpu as pltpu
from jax.sharding import PartitionSpec as P

HEADS = 64
HD = 128
ROPE = 64
LAT = 512
QW = HD + ROPE

theta_base = 10000.0
epsilon = 1e-06
masked_fill = -1e30
MESH = pl.DeviceIdType.MESH


def row_positions(order_ref, shape, axis, block_width, blocks):
    index = lax.broadcasted_iota(jnp.int32, shape, axis)
    block = index // block_width
    position = index - block * block_width
    for j in range(blocks):
        position = position + jnp.where(block == j, order_ref[0, j] * block_width, 0)
    return position


def attention_kernel(
    groups,
    lines,
    chunk_heads,
    order_ref,
    offset_ref,
    length_ref,
    owners_ref,
    gain_ref,
    frequency_ref,
    kv_ref,
    q_hbm,
    w_hbm,
    out_hbm,
    shipped_ref,
    qbuf,
    wbuf,
    raw,
    keys,
    pages,
    cos_ref,
    sin_ref,
    cache_t,
    rope_t,
    bias,
    obuf,
    w_sem,
    qown_sem,
    oown_sem,
    key_send,
    key_recv,
    q_send,
    q_recv,
    o_send,
    o_recv,
    line_send,
    line_recv,
    side_send,
    side_recv,
    core_send,
    core_recv,
):
    me = lax.axis_index("ctx")
    request = lax.axis_index("req")
    along, across = lines
    core = lax.rem(request, 2)
    side = lax.rem(request // 2, across)
    line = request // (2 * across)
    rows = q_hbm.shape[0]
    segment = rows * groups
    heads = w_hbm.shape[0]
    chunks = heads // chunk_heads
    q_width = chunk_heads * QW
    o_width = chunk_heads * HD
    blocks = order_ref.shape[1]
    block_width = segment // blocks

    def device(line_at, side_at, core_at):
        return {"req": (line_at * across + side_at) * 2 + core_at}

    def line_peer(step):
        return device(lax.rem(line + step, along), side, core)

    def side_peer(step):
        return device(line, lax.rem(side + step, across), core)

    def core_peer():
        return device(line, side, 1 - core)

    def line_copy(step):
        piece = pages.at[pl.ds((core * across + side) * along + line, 1)]
        return pltpu.make_async_remote_copy(
            src_ref=piece,
            dst_ref=piece,
            send_sem=line_send.at[step - 1],
            recv_sem=line_recv.at[step - 1],
            device_id=line_peer(step),
            device_id_type=MESH,
        )

    def side_copy(step):
        piece = pages.at[pl.ds((core * across + side) * along, along)]
        return pltpu.make_async_remote_copy(
            src_ref=piece,
            dst_ref=piece,
            send_sem=side_send.at[step - 1],
            recv_sem=side_recv.at[step - 1],
            device_id=side_peer(step),
            device_id_type=MESH,
        )

    def core_copy():
        piece = pages.at[pl.ds(core * (across * along), across * along)]
        return pltpu.make_async_remote_copy(
            src_ref=piece,
            dst_ref=piece,
            send_sem=core_send.at[0],
            recv_sem=core_recv.at[0],
            device_id=core_peer(),
            device_id_type=MESH,
        )

    def peer(step):
        return lax.rem(me + step, groups)

    def own_rows(index):
        return pl.ds(pl.multiple_of(index * rows, rows), rows)

    def q_columns(group, c):
        return pl.ds(pl.multiple_of(group * (heads * QW) + c * q_width, 128), q_width)

    def o_columns(group, c):
        return pl.ds(pl.multiple_of(group * (heads * HD) + c * o_width, 128), o_width)

    def key_copy(step):
        return pltpu.make_async_remote_copy(
            src_ref=kv_ref,
            dst_ref=raw.at[own_rows(me)],
            send_sem=key_send.at[step - 1],
            recv_sem=key_recv.at[step - 1],
            device_id={"ctx": peer(step)},
            device_id_type=MESH,
        )

    def q_copy(step, c):
        return pltpu.make_async_remote_copy(
            src_ref=q_hbm.at[:, q_columns(peer(step), c)],
            dst_ref=qbuf.at[c, own_rows(me)],
            send_sem=q_send.at[step - 1, c],
            recv_sem=q_recv.at[step - 1, c],
            device_id={"ctx": peer(step)},
            device_id_type=MESH,
        )

    def o_copy(step, c):
        return pltpu.make_async_remote_copy(
            src_ref=obuf.at[c, own_rows(peer(step))],
            dst_ref=out_hbm.at[:, o_columns(me, c)],
            send_sem=o_send.at[step - 1, c],
            recv_sem=o_recv.at[step - 1, c],
            device_id={"ctx": peer(step)},
            device_id_type=MESH,
        )

    def q_own(c):
        return pltpu.make_async_copy(
            q_hbm.at[:, q_columns(me, c)], qbuf.at[c, own_rows(me)], qown_sem.at[c]
        )

    def w_copy(c):
        return pltpu.make_async_copy(
            w_hbm.at[pl.ds(c * chunk_heads, chunk_heads)], wbuf.at[c], w_sem.at[c]
        )

    def o_own(c):
        return pltpu.make_async_copy(
            obuf.at[c, own_rows(me)], out_hbm.at[:, o_columns(me, c)], oown_sem.at[c]
        )

    barrier = pltpu.get_barrier_semaphore()
    for step in range(1, groups):
        pl.semaphore_signal(
            barrier, inc=1, device_id={"ctx": peer(step)}, device_id_type=MESH
        )
    for step in range(1, along):
        pl.semaphore_signal(barrier, inc=1, device_id=line_peer(step), device_id_type=MESH)
    for step in range(1, across):
        pl.semaphore_signal(barrier, inc=1, device_id=side_peer(step), device_id_type=MESH)
    pl.semaphore_signal(barrier, inc=1, device_id=core_peer(), device_id_type=MESH)
    pl.semaphore_wait(barrier, groups + along + across - 2)

    for step in range(1, groups):
        key_copy(step).start()
    for c in range(chunks):
        for step in range(1, groups):
            q_copy(step, c).start()
    for c in range(chunks):
        w_copy(c).start()
        q_own(c).start()

    length = length_ref[0]
    row_pos = row_positions(order_ref, (segment, HD), 0, block_width, blocks)
    angles = (row_pos + offset_ref[0]).astype(jnp.float32) * frequency_ref[...]
    wide_lane = lax.broadcasted_iota(jnp.int32, (segment, HD), 1)
    cos_ref[...] = jnp.cos(angles)
    sine = jnp.sin(angles)
    sin_ref[...] = jnp.where((wide_lane & (ROPE // 2)) == 0, -sine, sine)

    def normalise(group):
        latent = raw[own_rows(group), :LAT].astype(jnp.float32)
        mean_square = jnp.mean(latent * latent, axis=-1, keepdims=True)
        normed = latent * lax.rsqrt(mean_square + epsilon) * gain_ref[...]
        keys[own_rows(group), :LAT] = normed.astype(jnp.bfloat16)
        tail = raw[own_rows(group), LAT:].astype(jnp.float32)
        crossed = jnp.concatenate([tail[:, ROPE // 2 :], tail[:, : ROPE // 2]], axis=1)
        turned = (
            tail * cos_ref[own_rows(group), :ROPE] + crossed * sin_ref[own_rows(group), :ROPE]
        )
        keys[own_rows(group), LAT:] = turned.astype(jnp.bfloat16)

    raw[own_rows(me)] = kv_ref[...]
    normalise(me)
    pages[(core * across + side) * along + line] = keys[own_rows(me)]
    for step in range(1, along):
        line_copy(step).start()

    query_pos = row_positions(order_ref, (segment, 1), 0, block_width, blocks)
    key_pos = row_positions(order_ref, (1, segment), 1, block_width, blocks)
    bias[...] = jnp.where((key_pos <= query_pos) & (key_pos < length), 0.0, masked_fill)

    for step in range(1, groups):
        key_copy(step).wait()
        normalise(peer(step))
    for g in range(groups):
        span = slice(g * rows, (g + 1) * rows)
        cache_t[:, span] = keys[span, :LAT].astype(jnp.float32).T.astype(jnp.bfloat16)
        turned = keys[span, LAT:].astype(jnp.float32)
        empty = jnp.zeros_like(turned)
        rope_t[0, :, span] = jnp.concatenate([turned, empty], axis=1).T.astype(jnp.bfloat16)
        rope_t[1, :, span] = jnp.concatenate([empty, turned], axis=1).T.astype(jnp.bfloat16)

    scale = (QW ** -0.5) * math.log2(math.e)
    tile = min(256, segment)
    lane = lax.broadcasted_iota(jnp.int32, (tile, 128), 1)
    low = lane < ROPE
    first = (lane & (ROPE // 2)) == 0

    def one_chunk(c, carry):
        @pl.when(c == chunks // 4)
        def _():
            for step in range(1, along):
                line_copy(step).wait()
            for step in range(1, across):
                side_copy(step).start()

        @pl.when(c == chunks * 3 // 4)
        def _():
            for step in range(1, across):
                side_copy(step).wait()
            core_copy().start()

        w_copy(c).wait()
        q_own(c).wait()
        for step in range(1, groups):
            q_copy(step, c).wait()
        weights = wbuf[c].reshape(chunk_heads * 2 * HD, LAT)
        expanded = jnp.dot(
            weights, cache_t[...], preferred_element_type=jnp.float32
        ).astype(jnp.bfloat16)
        ones = jnp.ones((HD, segment), jnp.bfloat16)
        for t in range(segment // tile):
            span = slice(t * tile, (t + 1) * tile)
            index = lax.broadcasted_iota(jnp.int32, (tile, HD), 0) + t * tile
            block = index // block_width
            valid = index - block * block_width
            for j in range(blocks):
                valid = valid + jnp.where(block == j, order_ref[0, j] * block_width, 0)
            valid = valid < length
            for pair in range(chunk_heads // 2):
                at = pair * 2 * QW
                part0 = qbuf[c, span, at : at + 128]
                part1 = qbuf[c, span, at + 128 : at + 256].astype(jnp.float32)
                part2 = qbuf[c, span, at + 256 : at + 384].astype(jnp.float32)
                plain = jnp.where(low, part1, part2)
                other = jnp.where(
                    first,
                    pltpu.roll(plain, 128 - ROPE // 2, 1),
                    pltpu.roll(plain, ROPE // 2, 1),
                )
                turned = (plain * cos_ref[span] + other * sin_ref[span]).astype(jnp.bfloat16)
                swapped = jnp.where(low, part2, part1).astype(jnp.bfloat16)
                for odd in range(2):
                    top = (pair * 2 + odd) * 2 * HD
                    key_t = expanded[top : top + HD]
                    value_t = expanded[top + HD : top + 2 * HD]
                    if odd:
                        key_t = jnp.concatenate(
                            [key_t[HD // 2 :], key_t[: HD // 2], rope_t[1]], axis=0
                        )
                        query = jnp.concatenate([swapped, turned], axis=1)
                    else:
                        key_t = jnp.concatenate([key_t, rope_t[0]], axis=0)
                        query = jnp.concatenate([part0, turned], axis=1)
                    scores = (
                        jnp.dot(query, key_t, preferred_element_type=jnp.float32) * scale
                        + bias[span]
                    )
                    top_score = jnp.max(scores, axis=-1, keepdims=True)
                    weight = jnp.exp2(scores - top_score).astype(jnp.bfloat16)
                    summed = lax.dot_general(
                        weight,
                        jnp.concatenate([value_t, ones], axis=0),
                        (((1,), (1,)), ((), ())),
                        preferred_element_type=jnp.float32,
                    )
                    result = jnp.where(valid, summed[:, :HD] / summed[:, HD:], 0.0)
                    column = (pair * 2 + odd) * HD
                    obuf[c, span, column : column + HD] = result.astype(jnp.bfloat16)
        for step in range(1, groups):
            o_copy(step, c).start()
        o_own(c).start()
        return carry

    lax.fori_loop(0, chunks, one_chunk, 0)

    core_copy().wait()
    count = 0
    picked = [jnp.zeros((block_width, keys.shape[1]), jnp.bfloat16) for _ in range(2)]
    for source in range(2 * across * along):
        slot = ((source % 2) * across + source // 2 % across) * along + source // (2 * across)
        for page in range(2):
            match = owners_ref[source, page] == request
            content = pages[slot, page * block_width : (page + 1) * block_width]
            for place in range(2):
                picked[place] = jnp.where(match & (count == place), content, picked[place])
            count = count + match.astype(jnp.int32)
    for place in range(2):
        shipped_ref[place] = picked[place]

    def finish(c, carry):
        o_own(c).wait()
        for step in range(1, groups):
            o_copy(step, c).wait()
        return carry

    lax.fori_loop(0, chunks, finish, 0)


def attention(q, kv, gain, kv_up, order, offset, length, owners):
    groups = lax.axis_size("ctx")
    requests = lax.axis_size("req")
    chips = requests // 2
    along = max(d for d in range(1, chips + 1) if chips % d == 0 and d * d <= 2 * chips)
    across = chips // along
    rows = q.shape[0]
    segment = rows * groups
    blocks = order.shape[1]
    block_width = segment // blocks
    heads = kv_up.shape[0]
    chunk_heads = min(4, heads)
    chunks = heads // chunk_heads
    half = ROPE // 2
    frequency = np.exp(
        np.float32(-math.log(theta_base)) * np.arange(half, dtype=np.float32) / np.float32(half)
    )
    frequency = np.tile(frequency.astype(np.float32), 2 * HD // ROPE)[None]
    in_vmem = pl.BlockSpec(memory_space=pltpu.VMEM)
    in_smem = pl.BlockSpec(memory_space=pltpu.SMEM)
    anywhere = pl.BlockSpec(memory_space=pl.ANY)
    dma = pltpu.SemaphoreType.DMA
    others = groups - 1
    return pl.pallas_call(
        functools.partial(attention_kernel, groups, (along, across), chunk_heads),
        out_shape=(
            jax.ShapeDtypeStruct((rows, HEADS * HD), jnp.bfloat16),
            jax.ShapeDtypeStruct((2, block_width, LAT + ROPE), jnp.bfloat16),
        ),
        in_specs=[in_smem] * 4 + [in_vmem] * 3 + [anywhere] * 2,
        out_specs=(anywhere, in_vmem),
        scratch_shapes=[
            pltpu.VMEM((chunks, segment, chunk_heads * QW), jnp.bfloat16),
            pltpu.VMEM((chunks, chunk_heads, 2 * HD, LAT), jnp.bfloat16),
            pltpu.VMEM((segment, LAT + ROPE), jnp.bfloat16),
            pltpu.VMEM((segment, LAT + ROPE), jnp.bfloat16),
            pltpu.VMEM((requests, rows, LAT + ROPE), jnp.bfloat16),
            pltpu.VMEM((segment, HD), jnp.float32),
            pltpu.VMEM((segment, HD), jnp.float32),
            pltpu.VMEM((LAT, segment), jnp.bfloat16),
            pltpu.VMEM((2, 2 * ROPE, segment), jnp.bfloat16),
            pltpu.VMEM((segment, segment), jnp.float32),
            pltpu.VMEM((chunks, segment, chunk_heads * HD), jnp.bfloat16),
            dma((chunks,)),
            dma((chunks,)),
            dma((chunks,)),
            dma((others,)),
            dma((others,)),
            dma((others, chunks)),
            dma((others, chunks)),
            dma((others, chunks)),
            dma((others, chunks)),
            dma((along - 1,)),
            dma((along - 1,)),
            dma((across - 1,)),
            dma((across - 1,)),
            dma((1,)),
            dma((1,)),
        ],
        compiler_params=pltpu.CompilerParams(
            collective_id=0, has_side_effects=True, vmem_limit_bytes=56 * 2**20
        ),
        cost_estimate=pl.CostEstimate(
            flops=2 * heads * segment * (2 * HD * LAT + 4 * HD * segment),
            bytes_accessed=2 * (2 * rows * HEADS * QW + heads * 2 * HD * LAT + rows * HEADS * HD),
            transcendentals=heads * segment * segment,
        ),
    )(order, offset, length, owners, gain, jnp.asarray(frequency), kv, q, kv_up)


def per_device(q_heads, kv_latent, latent_gain, kv_up, offsets, lengths, block_order, owners):
    attn_out, shipped = attention(
        q_heads[0],
        kv_latent[0],
        latent_gain[None],
        kv_up,
        block_order,
        offsets,
        lengths,
        owners,
    )
    return (attn_out[None], shipped.reshape(1, 2, -1))


def solution(mesh):
    in_specs = (
        P("req", "ctx", None),
        P("req", "ctx", None),
        P(),
        P("ctx", None, None),
        P("req"),
        P("req"),
        P("req", None),
        P(None, "ctx"),
    )
    out_specs = (P("req", "ctx", None), P("req", "ctx", None))
    return jax.shard_map(
        per_device, mesh=mesh, in_specs=in_specs, out_specs=out_specs, check_vma=False
    )
```
